32 devices in a mesh: ctx: 16 (over z, x, core), exp: 2 (over y).
Axes of the slice: x: 2, y: 2, z: 4, core: 2. Of those that a mesh axis runs over, the one named last changes fastest.
Arguments:
- queries: bfloat16 [1024, 6144], P('ctx', 'exp'), may hold values from -23 to 23
- projected_key_value: bfloat16 [1024, 2, 1024], P('ctx', None, 'exp'), may hold values from -6 to 6
- doc_ids: int32 [1024], P('ctx'), may hold values from 0 to 7, never falling along the last dimension, each value on 1 to 768 neighbouring positions
- residual_in: bfloat16 [1024, 6144], P('exp', 'ctx'), may hold values from -6 to 6
- out_proj: bfloat16 [6144, 6144], P('exp', 'ctx'), may hold values from -0.3125 to 0.3125
- norm_gain: bfloat16 [6144], P('ctx'), may hold values from 0.25 to 1.75
- expert_ids: int32 [1024, 2], replicated, may hold values from 0 to 7, all different within a row; in each aligned block of 512 rows (0 to 511, 512 to 1023, ...) at most 144 rows name the same one
- route_weights: float32 [1024, 2], replicated, may hold values from 0.2 to 1
- gate_proj: bfloat16 [8, 6144, 8192], P('exp', None, 'ctx'), may hold values from -0.078125 to 0.078125
- up_proj: bfloat16 [8, 6144, 8192], P('exp', None, 'ctx'), may hold values from -0.078125 to 0.078125
- down_proj: bfloat16 [8, 8192, 6144], P('exp', None, 'ctx'), may hold values from -0.0625 to 0.0625
Outputs:
- mixed: bfloat16 [1024, 6144], P('exp', 'ctx')
The draws below stay inside these ranges and needn't reach their ends.
Inputs may be any that keep to these rules, and one draw needn't show every extreme that they name: `expert_ids`: in each aligned block of 512 rows no expert is named by more than 144 rows, a bound that some block reaches; each row names 2 different experts. `doc_ids`: document numbers never fall along the window; a document has at most 768 positions and one has exactly that many.
All inputs are finite; a program needn't handle non-finite values.
Results may differ from the reference program's by a relative error of at most 0.018.
Values may be sent and summed in bfloat16 or wider, within the bound.
A program may use at most 192 MiB of HBM per device.

```python
import math
import jax
import jax.numpy as jnp
import numpy as np
from jax import lax

D = 6144
QUERY_HEADS = 48
KEY_VALUE_HEADS = 8
HEAD_WIDTH = 128
EXPERTS = 8
FF = 8192
TOPK = 2
DOCS = 8
WINDOW_LENGTH = 1024
ROWS_B = 512
CAP = 144
DOC_MOST = 768
N_EXP = 2


def draw_queries(key, part):
    head_groups = QUERY_HEADS // KEY_VALUE_HEADS
    value_columns = jnp.clip(jax.random.normal(jax.random.fold_in(key, 3), (WINDOW_LENGTH, KEY_VALUE_HEADS, head_groups, HEAD_WIDTH), jnp.float32), -6.0, 6.0)
    return value_columns.reshape(WINDOW_LENGTH, QUERY_HEADS * HEAD_WIDTH).astype(jnp.bfloat16)


def draw_projected_key_value(key, part):
    value_columns = jnp.clip(jax.random.normal(jax.random.fold_in(key, 4), (WINDOW_LENGTH, 2, KEY_VALUE_HEADS, HEAD_WIDTH), jnp.float32), -6.0, 6.0)
    return value_columns.reshape(WINDOW_LENGTH, 2, KEY_VALUE_HEADS * HEAD_WIDTH).astype(jnp.bfloat16)


def level_of(key, shape, cuts, smallest, high):
    factor_of, own = 1.0, jax.random.fold_in(key, 6)
    for dim, blocks in cuts:
        steps = jnp.exp(jax.random.uniform(jax.random.fold_in(own, dim), (blocks,), jnp.float32, smallest / len(cuts), high / len(cuts)))
        factor_of = factor_of * jnp.repeat(steps, shape[dim] // blocks).reshape([-1 if axis == dim else 1 for axis in range(len(shape))])
    return factor_of


def profile(count, total, reach, lean):
    loads = [(1 << 20) // math.isqrt(grade ** lean) + 1 for grade in range(2, count + 1)]
    rest, holding = total - reach - (count - 1), [1] * (count - 1)
    while rest > 0:
        movable = [i for i in range(count - 1) if holding[i] < reach]
        pool, left = sum([loads[i] for i in movable]), rest
        for i in movable:
            more = min(reach - holding[i], max(1, left * loads[i] // pool), rest)
            holding[i] = holding[i] + more
            rest = rest - more
    return np.array([reach] + holding)


def uneven(stream_key, count, total, limit, lean):
    if count == 2:
        one = jax.random.randint(stream_key, (), max(1, total - limit), min(limit, total - 1) + 1)
        return jnp.stack([one, total - one])
    sizes = jnp.asarray(profile(count, total, limit, lean), jnp.int32)
    couples = (count - 1) // 2
    source_of, receiver = sizes[1:1 + 2 * couples:2], sizes[2:2 + 2 * couples:2]
    room = jnp.minimum(source_of - 1, limit - receiver)
    shifted = jax.random.randint(jax.random.fold_in(stream_key, 1), (couples,), 0, 1 << 20) % (room + 1)
    sizes = sizes.at[1:1 + 2 * couples:2].set(source_of - shifted).at[2:2 + 2 * couples:2].set(receiver + shifted)
    return sizes[jax.random.permutation(jax.random.fold_in(stream_key, 2), count)]


def deal_out(rng, own, number, rows, count, top, bound, slope):
    ranking = jax.random.permutation(rng, count)
    heavy_load, ordinary = load_shares(count, rows * top, bound, slope, True), load_shares(count, rows * top, bound, slope, False)
    places = jnp.arange(count)

    def named(tallies, offset_by):
        used = int((tallies > 0).sum())
        fixed = max(1, used // 4)
        shifted = fixed + (places - fixed + offset_by * (used - fixed)) % max(1, count - fixed)
        return jnp.zeros((count,), jnp.int32).at[ranking[jnp.where(places < fixed, places, shifted)]].set(jnp.asarray(tallies, jnp.int32))

    tallies = jnp.where(number % 4 == 0, named(heavy_load, number // 4), named(ordinary, number - number // 4 - 1))
    mixed = jax.random.permutation(jax.random.fold_in(own, 3), count)
    giver, receiver = mixed[0:count // 2 * 2:2], mixed[1:count // 2 * 2:2]
    slack = jnp.minimum(tallies[giver] - 1, bound - tallies[receiver]) // 2
    slack = jnp.where((giver == ranking[0]) | (receiver == ranking[0]) | (tallies[receiver] == 0), 0, jnp.maximum(slack, 0))
    shifted = jax.random.randint(jax.random.fold_in(own, 4), (count // 2,), 0, 1 << 20) % (slack + 1)
    tallies = tallies.at[giver].add(-shifted).at[receiver].add(shifted)
    members = jnp.searchsorted(jnp.cumsum(tallies), jnp.arange(rows * top), side="right").astype(jnp.int32)
    grid = members.reshape(top, rows).T
    grid = grid[jax.random.permutation(jax.random.fold_in(own, 1), rows)]
    offset_by = jax.random.randint(jax.random.fold_in(own, 2), (rows, 1), 0, top)
    return jnp.take_along_axis(grid, (jnp.arange(top)[None, :] + offset_by) % top, axis=1)


def load_shares(count, total, limit, slope, full):
    loads = [(1 << 20) // math.isqrt(grade ** slope) + 1 for grade in range(1, count + 1)]
    largest = limit if full else min(limit, max(-(-total // count), total * loads[0] // sum(loads)))
    least = 1 if total - largest >= count - 1 else 0
    counts, surplus = [largest] + [least] * (count - 1), total - largest - least * (count - 1)
    while surplus > 0:
        free = [i for i in range(1, count) if counts[i] < largest] or [i for i in range(1, count) if counts[i] < limit]
        pool, remaining = sum([loads[i] for i in free]), surplus
        for i in free:
            extra = min(limit - counts[i], max(1, remaining * loads[i] // pool), surplus)
            counts[i] = counts[i] + extra
            surplus = surplus - extra
    return np.array(counts)


def normal_values(rng, dims, deviation, bound, cuts=(), kind=jnp.bfloat16):
    factor_of = level_of(rng, dims, cuts, -0.22, 0.18) if cuts else 1.0
    entries = jax.random.normal(rng, dims, jnp.float32) * deviation * factor_of
    return jnp.minimum(jnp.maximum(entries, -bound), bound).astype(kind)


def setup_inputs(seed: int = 0) -> dict:
    splits = jax.random.split(jax.random.key(seed), 12)
    queries = draw_queries(jax.random.fold_in(splits[11], 71), 0)
    projected_key_value = draw_projected_key_value(jax.random.fold_in(splits[11], 71), 0)
    doc_ids = jnp.searchsorted(jnp.cumsum(uneven(splits[2], DOCS, WINDOW_LENGTH, DOC_MOST, 1)), jnp.arange(WINDOW_LENGTH), side="right").astype(jnp.int32)
    residual_in = normal_values(splits[3], (WINDOW_LENGTH, D), 1.0, 6.0, ((0, 2), (1, 16)))
    out_proj = normal_values(splits[4], (QUERY_HEADS * HEAD_WIDTH, D), (QUERY_HEADS * HEAD_WIDTH // 16) ** -0.5, 0.3125, ((0, 2), (1, 16)))
    norm_gain = jnp.clip(1.0 + 0.15 * jax.random.normal(splits[5], (D,), jnp.float32), 0.25, 1.75).astype(jnp.bfloat16)
    expert_ids_keys = jax.random.split(jax.random.fold_in(splits[6], 1), WINDOW_LENGTH // ROWS_B)
    expert_ids_turns = jax.random.permutation(jax.random.fold_in(splits[6], 3), WINDOW_LENGTH // ROWS_B)
    expert_ids = jax.vmap(lambda own, number: deal_out(jax.random.fold_in(splits[6], 2), own, number, ROWS_B, EXPERTS, TOPK, CAP, 2))(expert_ids_keys, expert_ids_turns).reshape((WINDOW_LENGTH, TOPK))
    route_weights = jnp.clip(jax.random.uniform(splits[7], (WINDOW_LENGTH, TOPK), jnp.float32, 0.2, 1.0), 0.2, 1.0)
    gate_proj = normal_values(splits[8], (EXPERTS, D, FF), D ** -0.5, 0.078125, ((0, 2), (2, 16)))
    up_proj = normal_values(splits[9], (EXPERTS, D, FF), D ** -0.5, 0.078125, ((0, 2), (2, 16)))
    down_proj = normal_values(splits[10], (EXPERTS, FF, D), FF ** -0.5, 0.0625, ((0, 2), (2, 16)))
    return {"queries": queries, "projected_key_value": projected_key_value, "doc_ids": doc_ids, "residual_in": residual_in, "out_proj": out_proj, "norm_gain": norm_gain, "expert_ids": expert_ids, "route_weights": route_weights, "gate_proj": gate_proj, "up_proj": up_proj, "down_proj": down_proj}


NEG = -1e+30

def routing_tables(expert_ids, route_weights, n_experts, n_blocks):
    seq_len = expert_ids.shape[0]
    rows_block = seq_len // n_blocks
    capacity = rows_block * 9 // 32
    labels = jnp.arange(n_experts, dtype=jnp.int32)
    onehot = (expert_ids[:, :, None] == labels[None, None, :]).astype(jnp.int32)
    hits = lax.optimization_barrier(jnp.sum(onehot, axis=1)).reshape(n_blocks, rows_block, n_experts)
    before = (jnp.cumsum(hits, axis=1) - hits).reshape(seq_len, n_experts)
    rank = lax.optimization_barrier(jnp.sum(onehot * before[:, None, :], axis=2))
    position = jnp.arange(seq_len, dtype=jnp.int32)
    slot = (position // rows_block)[:, None] * capacity + rank
    width = n_blocks * capacity
    owners = jnp.broadcast_to(position[:, None], expert_ids.shape).astype(jnp.int32)
    tok_of = jnp.zeros((n_experts, width), jnp.int32).at[expert_ids, slot].set(owners)
    valid = jnp.zeros((n_experts, width), jnp.float32).at[expert_ids, slot].set(1.0)
    weight = jnp.zeros((n_experts, width), jnp.float32).at[expert_ids, slot].set(route_weights.astype(jnp.float32))
    first = jnp.zeros((n_experts, width), jnp.float32).at[expert_ids[:, 0], slot[:, 0]].set(1.0)
    return (tok_of, valid, weight, first)

def reference(queries, projected_key_value, doc_ids, residual_in, out_proj, norm_gain, expert_ids, route_weights, gate_proj, up_proj, down_proj):
    head_groups = QUERY_HEADS // KEY_VALUE_HEADS
    scale = 1.0 / math.sqrt(HEAD_WIDTH)
    position = jnp.arange(WINDOW_LENGTH, dtype=jnp.int32)
    visible = (doc_ids[:, None] == doc_ids[None, :]) & (position[None, :] <= position[:, None])
    heads_of_queries = queries.reshape(WINDOW_LENGTH, KEY_VALUE_HEADS, head_groups, HEAD_WIDTH).transpose(1, 0, 2, 3)
    heads_of_keys = projected_key_value[:, 0].reshape(WINDOW_LENGTH, KEY_VALUE_HEADS, HEAD_WIDTH).transpose(1, 0, 2)
    heads_of_values = projected_key_value[:, 1].reshape(WINDOW_LENGTH, KEY_VALUE_HEADS, HEAD_WIDTH).transpose(1, 0, 2)

    def one_head(items):
        query_h, key_h, value_h = items
        scores = jnp.einsum('tgd,sd->gts', query_h.astype(jnp.float32), key_h.astype(jnp.float32)) * scale
        scores = jnp.where(visible[None], scores, NEG)
        top = lax.optimization_barrier(jnp.max(scores, axis=-1, keepdims=True))
        expo = jnp.where(visible[None], jnp.exp(scores - top), 0.0)
        total = lax.optimization_barrier(jnp.sum(expo, axis=-1))
        weights = expo.astype(jnp.bfloat16)
        attended = jnp.einsum('gts,sd->gtd', weights.astype(jnp.float32), value_h.astype(jnp.float32))
        return (attended / total[..., None]).astype(jnp.bfloat16)
    heads = lax.map(one_head, (heads_of_queries, heads_of_keys, heads_of_values))
    attended = heads.transpose(2, 0, 1, 3).reshape(WINDOW_LENGTH, QUERY_HEADS * HEAD_WIDTH)
    head_out = jnp.dot(attended, out_proj, preferred_element_type=jnp.float32)
    stream = (residual_in.astype(jnp.float32) + head_out).astype(jnp.bfloat16)
    tok_of, valid, weight, first = routing_tables(expert_ids, route_weights, EXPERTS, N_EXP)
    gain_f = norm_gain.astype(jnp.float32)

    def per_expert(result, items):
        tokens, live, wts, lead, w_gate, w_up, w_down = items
        rows = jnp.where(live[:, None] > 0, stream[tokens], jnp.zeros((), jnp.bfloat16))
        rows_f = rows.astype(jnp.float32)
        meansq = lax.optimization_barrier(jnp.mean(rows_f * rows_f, axis=-1, keepdims=True))
        normed = (rows_f * lax.rsqrt(meansq + 1e-05) * gain_f).astype(jnp.bfloat16)
        gate = jnp.dot(normed, w_gate, preferred_element_type=jnp.float32)
        upper = jnp.dot(normed, w_up, preferred_element_type=jnp.float32)
        hidden = (jax.nn.silu(gate) * upper).astype(jnp.bfloat16)
        expert_out = jnp.dot(hidden, w_down, preferred_element_type=jnp.float32)
        contrib = wts[:, None] * expert_out + lead[:, None] * rows_f
        return (result.at[tokens].add(contrib * live[:, None]), None)
    result, unused = lax.scan(per_expert, jnp.zeros((WINDOW_LENGTH, D), jnp.float32), (tok_of, valid, weight, first, gate_proj, up_proj, down_proj))
    return result.astype(jnp.bfloat16)
```

```python
import functools
import math

import jax
import jax.numpy as jnp
from jax import lax
from jax.experimental import pallas as pl
from jax.experimental.pallas import tpu as pltpu
from jax.sharding import PartitionSpec as P

QUERY_HEADS = 48
KEY_VALUE_HEADS = 8
HEAD_WIDTH = 128
EXPERTS = 8
NEG = -1e30

CHIPS = 8
RING_SIZE = 2 * CHIPS
MIB = 1 << 20


def chip_of(pos):
    x = pos // 4
    z = pos * (1 - x) + (CHIPS - 1 - pos) * x
    return z * 2 + x


def ring_place():
    me = lax.axis_index("ctx")
    core = lax.rem(me, 2)
    x = lax.rem(me // 2, 2)
    z = me // 4
    return z * (1 - x) + (CHIPS - 1 - z) * x, core


def ring_gather(x_ref, buf, sems, consume=None, ahead=None):
    local_sem, send_r, recv_r, send_l, recv_l, send_s, recv_s = sems
    pos, core = ring_place()

    def at(offset, c):
        return chip_of(lax.rem(pos + offset + CHIPS, CHIPS)) * 2 + c

    me = at(0, core)
    right, left, sibling = at(1, core), at(-1, core), at(0, 1 - core)
    half = x_ref.shape[0] // 2

    own = pltpu.make_async_copy(x_ref, buf.at[me], local_sem)
    own.start()
    barrier = pltpu.get_barrier_semaphore()
    for other in (right, left, sibling):
        pl.semaphore_signal(
            barrier, inc=1, device_id={"ctx": other}, device_id_type=pl.DeviceIdType.MESH
        )
    if ahead is not None:
        ahead(me)
    pl.semaphore_wait(barrier, 3)
    own.wait()

    def copy(origin, target, send, recv, part=None):
        view = buf.at[origin]
        if part is not None:
            view = buf.at[origin, pl.ds(part * half, half)]
        return pltpu.make_async_remote_copy(
            src_ref=view,
            dst_ref=view,
            send_sem=send,
            recv_sem=recv,
            device_id={"ctx": target},
            device_id_type=pl.DeviceIdType.MESH,
        )

    def to_right(k):
        return copy(at(1 - k, core), right, send_r.at[k - 1], recv_r.at[k - 1], 0 if k == 4 else None)

    def from_left(k):
        return copy(at(-k, core), right, send_r.at[k - 1], recv_r.at[k - 1], 0 if k == 4 else None)

    def to_left(k):
        return copy(at(k - 1, core), left, send_l.at[k - 1], recv_l.at[k - 1], 1 if k == 4 else None)

    def from_right(k):
        return copy(at(k, core), left, send_l.at[k - 1], recv_l.at[k - 1], 1 if k == 4 else None)

    def to_sibling(n, offset):
        return copy(at(offset, core), sibling, send_s.at[n], recv_s.at[n])

    def from_sibling(n, offset):
        return copy(at(offset, 1 - core), sibling, send_s.at[n], recv_s.at[n])

    order = [(0, 0), (-1, 0), (1, 0), (0, 1)]
    order += [(-2, 0), (2, 0), (-1, 1), (1, 1)]
    order += [(-3, 0), (3, 0), (-2, 1), (2, 1), (-3, 1), (3, 1), (4, 0), (4, 1)]
    number = {0: 0, -1: 1, 1: 2, -2: 3, 2: 4, -3: 5, 3: 6, 4: 7}

    def place(step):
        offset, other = order[step]
        return at(offset, 1 - core if other else core)

    def use(step):
        offset, other = order[step]
        if other:
            from_sibling(number[offset], offset).wait_recv()
        if consume is not None:
            consume(step, place(step), place(step + 1) if step + 1 < len(order) else None)

    to_right(1).start()
    to_left(1).start()
    to_sibling(0, 0).start()
    use(0)
    step = 1
    for k in (1, 2, 3):
        from_left(k).wait_recv()
        to_right(k + 1).start()
        to_sibling(number[-k], -k).start()
        from_right(k).wait_recv()
        to_left(k + 1).start()
        to_sibling(number[k], k).start()
        count = (3, 4, 6)[k - 1]
        for _ in range(count):
            use(step)
            step += 1
    from_left(4).wait_recv()
    from_right(4).wait_recv()
    to_sibling(7, 4).start()
    use(14)
    use(15)
    for k in (1, 2, 3, 4):
        to_right(k).wait_send()
        to_left(k).wait_send()
    for offset, n in number.items():
        to_sibling(n, offset).wait_send()


RING_SEMS = [
    pltpu.SemaphoreType.DMA,
    pltpu.SemaphoreType.DMA((4,)),
    pltpu.SemaphoreType.DMA((4,)),
    pltpu.SemaphoreType.DMA((4,)),
    pltpu.SemaphoreType.DMA((4,)),
    pltpu.SemaphoreType.DMA((8,)),
    pltpu.SemaphoreType.DMA((8,)),
]
VMEM_REF = pl.BlockSpec(memory_space=pltpu.VMEM)
ANY_REF = pl.BlockSpec(memory_space=pl.ANY)


def gather_kernel(x_ref, out_ref, *sems):
    ring_gather(x_ref, out_ref, sems)


def gathered_rows(x, collective_id):
    out = pl.pallas_call(
        gather_kernel,
        out_shape=jax.ShapeDtypeStruct((RING_SIZE,) + x.shape, x.dtype),
        in_specs=[ANY_REF],
        out_specs=ANY_REF,
        scratch_shapes=RING_SEMS,
        compiler_params=pltpu.CompilerParams(collective_id=collective_id, has_side_effects=True),
    )(x)
    return out.reshape((RING_SIZE * x.shape[0],) + x.shape[1:])


def weight_chunk(w_ref, wbuf, sem, origin, slot):
    depth = wbuf.shape[2]
    rows = pl.ds(pl.multiple_of(origin * depth, depth), depth)
    return pltpu.make_async_copy(w_ref.at[:, rows, :], wbuf.at[slot], sem.at[slot])


def hidden_kernel(width, x_ref, gain_ref, gate_ref, up_ref, out_ref, buf, wg, wu, ag, au, ss, wsem_g, wsem_u, *sems):
    experts = buf.shape[1]

    def fetch(origin, slot):
        weight_chunk(gate_ref, wg, wsem_g, origin, slot).start()
        weight_chunk(up_ref, wu, wsem_u, origin, slot).start()

    def consume(step, origin, following):
        slot = step % 2
        weight_chunk(gate_ref, wg, wsem_g, origin, slot).wait()
        weight_chunk(up_ref, wu, wsem_u, origin, slot).wait()
        if following is not None:
            fetch(following, 1 - slot)
        gain = gain_ref[origin]

        def one(e, carry):
            xf = buf[origin, e].astype(jnp.float32)
            xg = (xf * gain).astype(jnp.bfloat16)
            squares = jnp.sum(xf * xf, axis=-1, keepdims=True)
            g = jnp.dot(xg, wg[slot, e], preferred_element_type=jnp.float32)
            u = jnp.dot(xg, wu[slot, e], preferred_element_type=jnp.float32)
            if step == 0:
                ss[e] = squares
                ag[e] = g
                au[e] = u
            else:
                ss[e] += squares
                ag[e] += g
                au[e] += u
            return carry

        lax.fori_loop(0, experts, one, 0)

    ring_gather(x_ref, buf, sems, consume, lambda me: fetch(me, 0))

    def finish(e, carry):
        inverse = lax.rsqrt(ss[e] / width + 1e-05)
        g = ag[e] * inverse
        u = au[e] * inverse
        out_ref[e] = (g / (1.0 + jnp.exp(-g)) * u).astype(out_ref.dtype)
        return carry

    lax.fori_loop(0, experts, finish, 0)


def ring_hidden(rows, gain, gate_proj, up_proj):
    experts, count, depth = rows.shape
    units = gate_proj.shape[2]
    return pl.pallas_call(
        functools.partial(hidden_kernel, gate_proj.shape[1]),
        out_shape=jax.ShapeDtypeStruct((experts, count, units), jnp.bfloat16),
        in_specs=[ANY_REF, VMEM_REF, ANY_REF, ANY_REF],
        out_specs=VMEM_REF,
        scratch_shapes=[
            pltpu.VMEM((RING_SIZE, experts, count, depth), jnp.bfloat16),
            pltpu.VMEM((2, experts, depth, units), jnp.bfloat16),
            pltpu.VMEM((2, experts, depth, units), jnp.bfloat16),
            pltpu.VMEM((experts, count, units), jnp.float32),
            pltpu.VMEM((experts, count, units), jnp.float32),
            pltpu.VMEM((experts, count, 1), jnp.float32),
            pltpu.SemaphoreType.DMA((2,)),
            pltpu.SemaphoreType.DMA((2,)),
        ]
        + RING_SEMS,
        compiler_params=pltpu.CompilerParams(
            collective_id=2, has_side_effects=True, vmem_limit_bytes=48 * MIB
        ),
    )(rows, gain, gate_proj, up_proj)


def down_kernel(x_ref, down_ref, out_ref, buf, wd, wsem, *sems):
    experts = buf.shape[1]

    def consume(step, origin, following):
        slot = step % 2
        weight_chunk(down_ref, wd, wsem, origin, slot).wait()
        if following is not None:
            weight_chunk(down_ref, wd, wsem, following, 1 - slot).start()

        def one(e, carry):
            y = jnp.dot(buf[origin, e], wd[slot, e], preferred_element_type=jnp.float32)
            if step == 0:
                out_ref[e] = y
            else:
                out_ref[e] += y
            return carry

        lax.fori_loop(0, experts, one, 0)

    ring_gather(
        x_ref, buf, sems, consume, lambda me: weight_chunk(down_ref, wd, wsem, me, 0).start()
    )


def ring_down(hidden, down_proj):
    experts, count, depth = hidden.shape
    features = down_proj.shape[2]
    return pl.pallas_call(
        down_kernel,
        out_shape=jax.ShapeDtypeStruct((experts, count, features), jnp.float32),
        in_specs=[ANY_REF, ANY_REF],
        out_specs=VMEM_REF,
        scratch_shapes=[
            pltpu.VMEM((RING_SIZE, experts, count, depth), jnp.bfloat16),
            pltpu.VMEM((2, experts, depth, features), jnp.bfloat16),
            pltpu.SemaphoreType.DMA((2,)),
        ]
        + RING_SEMS,
        compiler_params=pltpu.CompilerParams(
            collective_id=3, has_side_effects=True, vmem_limit_bytes=48 * MIB
        ),
    )(hidden, down_proj)


def slot_ranks(expert_ids, n_experts, n_blocks):
    seq_len = expert_ids.shape[0]
    rows_block = seq_len // n_blocks
    labels = jnp.arange(n_experts, dtype=jnp.int32)
    onehot = (expert_ids[:, :, None] == labels[None, None, :]).astype(jnp.int32)
    hits = jnp.sum(onehot, axis=1).reshape(n_blocks, rows_block, n_experts)
    before = (jnp.cumsum(hits, axis=1) - hits).reshape(seq_len, n_experts)
    return jnp.sum(onehot * before[:, None, :], axis=2)


def on_device(
    ring,
    queries,
    projected_key_value,
    doc_ids,
    residual_in,
    out_proj,
    norm_gain,
    expert_ids,
    route_weights,
    gate_proj,
    up_proj,
    down_proj,
):
    def gather(x, collective_id):
        if ring:
            return gathered_rows(x, collective_id)
        return lax.all_gather(x, "ctx", axis=0, tiled=True)

    tok_count = queries.shape[0]
    head_groups = QUERY_HEADS // KEY_VALUE_HEADS
    kv_width = projected_key_value.shape[2]
    kv_local = kv_width // HEAD_WIDTH
    scale = 1.0 / math.sqrt(HEAD_WIDTH)
    heads_of_queries = queries.reshape(tok_count, kv_local, head_groups, HEAD_WIDTH)
    query_pos = lax.axis_index("ctx") * tok_count + jnp.arange(tok_count, dtype=jnp.int32)

    feat_local = norm_gain.shape[0]
    per_row = -(-feat_local // tok_count)
    gain_cols = jnp.pad(norm_gain, (0, per_row * tok_count - feat_local)).reshape(tok_count, per_row)
    side = jnp.concatenate([doc_ids.astype(jnp.bfloat16)[:, None], gain_cols], axis=1)
    side = jnp.pad(side, ((0, 0), (0, HEAD_WIDTH - 1 - per_row)))
    packed = jnp.concatenate([projected_key_value.reshape(tok_count, 2 * kv_width), side], axis=1)
    piece = gather(packed, 0)
    key_rows = piece.shape[0]
    ctx_size = key_rows // tok_count
    doc_piece = piece[:, 2 * kv_width].astype(jnp.int32)
    gain_piece = piece[:, 2 * kv_width + 1 : 2 * kv_width + 1 + per_row]
    gain_full = gain_piece.reshape(ctx_size, tok_count * per_row)[:, :feat_local].astype(jnp.float32)
    heads_of_keys = piece[:, :kv_width].reshape(key_rows, kv_local, HEAD_WIDTH)
    heads_of_values = piece[:, kv_width : 2 * kv_width].reshape(key_rows, kv_local, HEAD_WIDTH)
    key_pos = jnp.arange(key_rows, dtype=jnp.int32)
    visible = (doc_ids[:, None] == doc_piece[None, :]) & (key_pos[None, :] <= query_pos[:, None])
    scores = (
        jnp.einsum(
            "tkgd,skd->kgts", heads_of_queries, heads_of_keys, preferred_element_type=jnp.float32
        )
        * scale
    )
    scores = jnp.where(visible, scores, NEG)
    top = jnp.max(scores, axis=-1)
    expo = jnp.where(visible, jnp.exp(scores - top[..., None]), 0.0)
    total_new = jnp.sum(expo, axis=-1)
    weights = expo.astype(jnp.bfloat16)
    product = jnp.einsum(
        "kgts,skd->kgtd", weights, heads_of_values, preferred_element_type=jnp.float32
    )
    attended = (
        (product / total_new[..., None])
        .transpose(2, 0, 1, 3)
        .reshape(tok_count, -1)
        .astype(jnp.bfloat16)
    )
    partial_out = jnp.dot(gather(attended, 1), out_proj, preferred_element_type=jnp.float32)

    n_blocks = lax.axis_size("exp")
    block_index = lax.axis_index("exp")
    seq_len = expert_ids.shape[0]
    rows_block = seq_len // n_blocks
    capacity = rows_block * 9 // 32
    width = n_blocks * capacity
    local_experts = gate_proj.shape[0]
    rank = slot_ranks(expert_ids, EXPERTS, n_blocks)
    position = jnp.arange(seq_len, dtype=jnp.int32)
    slot_key = expert_ids * width + (position // rows_block)[:, None] * capacity + rank
    own_rows = lax.dynamic_slice_in_dim(
        partial_out, block_index * rows_block, rows_block, 0
    ) + residual_in.astype(jnp.float32)
    with_base = lax.dynamic_update_slice_in_dim(
        partial_out, own_rows, block_index * rows_block, 0
    ).astype(jnp.bfloat16)
    slots = jnp.arange(EXPERTS * width, dtype=jnp.int32)[:, None]
    chosen = ((slots == slot_key[None, :, 0]) | (slots == slot_key[None, :, 1])).astype(jnp.bfloat16)
    shares = jnp.dot(chosen, with_base, preferred_element_type=jnp.float32)
    received = lax.all_to_all(
        shares.astype(jnp.bfloat16).reshape(EXPERTS, width, feat_local),
        "exp",
        split_axis=0,
        concat_axis=1,
        tiled=True,
    ).astype(jnp.float32)
    expert_rows = jnp.sum(
        received.reshape(local_experts, n_blocks, -1, feat_local), axis=1
    ).astype(jnp.bfloat16)

    my_slots = block_index * local_experts * width + jnp.arange(local_experts * width, dtype=jnp.int32)
    lead = my_slots[:, None] == slot_key[None, :, 0]
    second = my_slots[:, None] == slot_key[None, :, 1]
    my_weight = jnp.sum(
        jnp.where(lead, route_weights[None, :, 0], jnp.where(second, route_weights[None, :, 1], 0.0)),
        axis=1,
    ).reshape(local_experts, width)
    my_first = jnp.sum(lead.astype(jnp.float32), axis=1).reshape(local_experts, width)

    if ring:
        hidden = ring_hidden(expert_rows, gain_full[:, None, :], gate_proj, up_proj)
        expert_out = ring_down(hidden, down_proj)
    else:
        full_rows = lax.all_gather(expert_rows, "ctx", axis=2, tiled=True)
        meansq = (
            jnp.einsum("erd,erd->er", full_rows, full_rows, preferred_element_type=jnp.float32)
            / full_rows.shape[2]
        )
        inverse = lax.rsqrt(meansq + 1e-05)
        normed = (
            full_rows.astype(jnp.float32) * inverse[..., None] * gain_full.reshape(-1)
        ).astype(jnp.bfloat16)
        gate = jnp.einsum("erd,edf->erf", normed, gate_proj, preferred_element_type=jnp.float32)
        upper = jnp.einsum("erd,edf->erf", normed, up_proj, preferred_element_type=jnp.float32)
        hidden = (jax.nn.silu(gate) * upper).astype(jnp.bfloat16)
        expert_out = jnp.einsum(
            "erf,efd->erd",
            lax.all_gather(hidden, "ctx", axis=2, tiled=True),
            down_proj,
            preferred_element_type=jnp.float32,
        )
    payload = my_weight[..., None] * expert_out + my_first[..., None] * expert_rows.astype(
        jnp.float32
    )
    back = lax.all_to_all(
        payload.reshape(local_experts, n_blocks, capacity, feat_local).astype(jnp.bfloat16),
        "exp",
        split_axis=1,
        concat_axis=0,
        tiled=True,
    )
    back = back.reshape(EXPERTS * capacity, feat_local)
    block_key = lax.dynamic_slice_in_dim(
        expert_ids * capacity + rank, block_index * rows_block, rows_block, 0
    )
    labels = jnp.arange(EXPERTS * capacity, dtype=jnp.int32)[None, :]
    picker = ((labels == block_key[:, :1]) | (labels == block_key[:, 1:])).astype(jnp.bfloat16)
    mixed = jnp.dot(picker, back, preferred_element_type=jnp.float32)
    return mixed.astype(jnp.bfloat16)


def solution(mesh):
    ring = mesh.shape["ctx"] == RING_SIZE
    placed = (
        P("ctx", "exp"),
        P("ctx", None, "exp"),
        P("ctx"),
        P("exp", "ctx"),
        P("exp", "ctx"),
        P("ctx"),
        P(),
        P(),
        P("exp", None, "ctx"),
        P("exp", None, "ctx"),
        P("exp", None, "ctx"),
    )
    return jax.shard_map(
        functools.partial(on_device, ring),
        mesh=mesh,
        in_specs=placed,
        out_specs=P("exp", "ctx"),
        check_vma=False,
    )
```

```python
import functools
import math

import jax
import jax.numpy as jnp
from jax import lax
from jax.experimental import pallas as pl
from jax.experimental.pallas import tpu as pltpu
from jax.sharding import PartitionSpec as P

QUERY_HEADS = 48
KEY_VALUE_HEADS = 8
HEAD_WIDTH = 128
EXPERTS = 8
NEG = -1e30

CHIPS = 8
RING_SIZE = 2 * CHIPS
MIB = 1 << 20


def chip_of(pos):
    x = pos // 4
    z = pos * (1 - x) + (CHIPS - 1 - pos) * x
    return z * 2 + x


def ring_place():
    me = lax.axis_index("ctx")
    core = lax.rem(me, 2)
    x = lax.rem(me // 2, 2)
    z = me // 4
    return z * (1 - x) + (CHIPS - 1 - z) * x, core


def ring_gather(x_ref, buf, sems, consume=None, ahead=None):
    local_sem, send_r, recv_r, send_l, recv_l, send_s, recv_s = sems
    pos, core = ring_place()

    def at(offset, c):
        return chip_of(lax.rem(pos + offset + CHIPS, CHIPS)) * 2 + c

    me = at(0, core)
    right, left, sibling = at(1, core), at(-1, core), at(0, 1 - core)
    half = x_ref.shape[0] // 2

    own = pltpu.make_async_copy(x_ref, buf.at[me], local_sem)
    own.start()
    barrier = pltpu.get_barrier_semaphore()
    for other in (right, left, sibling):
        pl.semaphore_signal(
            barrier, inc=1, device_id={"ctx": other}, device_id_type=pl.DeviceIdType.MESH
        )
    if ahead is not None:
        ahead(me)
    pl.semaphore_wait(barrier, 3)
    own.wait()

    def copy(origin, target, send, recv, part=None):
        view = buf.at[origin]
        if part is not None:
            view = buf.at[origin, pl.ds(part * half, half)]
        return pltpu.make_async_remote_copy(
            src_ref=view,
            dst_ref=view,
            send_sem=send,
            recv_sem=recv,
            device_id={"ctx": target},
            device_id_type=pl.DeviceIdType.MESH,
        )

    def rightward(k, part, sent):
        n = 2 * (k - 1) + part
        return copy(at(1 - k if sent else -k, core), right, send_r.at[n], recv_r.at[n], part)

    def leftward(k, part, sent):
        n = 2 * (k - 1) + part
        return copy(at(k - 1 if sent else k, core), left, send_l.at[n], recv_l.at[n], part)

    def to_sibling(n, offset):
        return copy(at(offset, core), sibling, send_s.at[n], recv_s.at[n])

    def from_sibling(n, offset):
        return copy(at(offset, 1 - core), sibling, send_s.at[n], recv_s.at[n])

    order = [(0, 0), (-1, 0), (1, 0), (0, 1)]
    order += [(-2, 0), (2, 0), (-1, 1), (1, 1)]
    order += [(-3, 0), (3, 0), (-2, 1), (2, 1), (-3, 1), (3, 1), (4, 0), (4, 1)]
    number = {0: 0, -1: 1, 1: 2, -2: 3, 2: 4, -3: 5, 3: 6, 4: 7}

    def place(step):
        offset, other = order[step]
        return at(offset, 1 - core if other else core)

    def use(step):
        offset, other = order[step]
        if other:
            from_sibling(number[offset], offset).wait_recv()
        if consume is not None:
            consume(step, place(step), place(step + 1) if step + 1 < len(order) else None)

    rightward(1, 0, True).start()
    leftward(1, 1, True).start()
    rightward(1, 1, True).start()
    leftward(1, 0, True).start()
    to_sibling(0, 0).start()
    before = {1: (0,), 2: (1, 2), 3: (4, 5)}
    between = {1: (), 2: (3,), 3: (6, 7)}
    for k in (1, 2, 3):
        for step in before[k]:
            use(step)
        rightward(k, 0, False).wait_recv()
        rightward(k + 1, 0, True).start()
        leftward(k, 1, False).wait_recv()
        leftward(k + 1, 1, True).start()
        for step in between[k]:
            use(step)
        rightward(k, 1, False).wait_recv()
        if k < 3:
            rightward(k + 1, 1, True).start()
        to_sibling(number[-k], -k).start()
        leftward(k, 0, False).wait_recv()
        if k < 3:
            leftward(k + 1, 0, True).start()
        to_sibling(number[k], k).start()
    for step in (8, 9, 10, 11):
        use(step)
    rightward(4, 0, False).wait_recv()
    leftward(4, 1, False).wait_recv()
    to_sibling(7, 4).start()
    for step in (12, 13, 14, 15):
        use(step)
    for k in (1, 2, 3, 4):
        rightward(k, 0, True).wait_send()
        leftward(k, 1, True).wait_send()
        if k < 4:
            rightward(k, 1, True).wait_send()
            leftward(k, 0, True).wait_send()
    for offset, n in number.items():
        to_sibling(n, offset).wait_send()


RING_SEMS = [
    pltpu.SemaphoreType.DMA,
    pltpu.SemaphoreType.DMA((8,)),
    pltpu.SemaphoreType.DMA((8,)),
    pltpu.SemaphoreType.DMA((8,)),
    pltpu.SemaphoreType.DMA((8,)),
    pltpu.SemaphoreType.DMA((8,)),
    pltpu.SemaphoreType.DMA((8,)),
]
VMEM_REF = pl.BlockSpec(memory_space=pltpu.VMEM)
ANY_REF = pl.BlockSpec(memory_space=pl.ANY)


def gather_kernel(x_ref, out_ref, *sems):
    ring_gather(x_ref, out_ref, sems)


def gathered_rows(x):
    out = pl.pallas_call(
        gather_kernel,
        out_shape=jax.ShapeDtypeStruct((RING_SIZE,) + x.shape, x.dtype),
        in_specs=[ANY_REF],
        out_specs=VMEM_REF,
        scratch_shapes=RING_SEMS,
        compiler_params=pltpu.CompilerParams(
            collective_id=0, has_side_effects=True, vmem_limit_bytes=16 * MIB
        ),
    )(x)
    return out.reshape((RING_SIZE * x.shape[0],) + x.shape[1:])


def project_kernel(x_ref, w_ref, out_ref, buf, *sems):
    ring_gather(x_ref, buf, sems)
    shards = 4
    rows = shards * x_ref.shape[0]
    for group in range(RING_SIZE // shards):
        x = buf[pl.ds(group * shards, shards)].reshape(rows, x_ref.shape[1])
        out_ref[pl.ds(group * rows, rows), :] = jnp.dot(
            x, w_ref[...], preferred_element_type=jnp.float32
        )


def ring_project(x, weight):
    return pl.pallas_call(
        project_kernel,
        out_shape=jax.ShapeDtypeStruct((RING_SIZE * x.shape[0], weight.shape[1]), jnp.float32),
        in_specs=[ANY_REF, VMEM_REF],
        out_specs=VMEM_REF,
        scratch_shapes=[pltpu.VMEM((RING_SIZE,) + x.shape, x.dtype)] + RING_SEMS,
        compiler_params=pltpu.CompilerParams(
            collective_id=1, has_side_effects=True, vmem_limit_bytes=40 * MIB
        ),
    )(x, weight)


def attention_kernel(scale, q_ref, kv_ref, bias_ref, out_ref):
    count, width = q_ref.shape[0], HEAD_WIDTH
    group = QUERY_HEADS // KEY_VALUE_HEADS
    heads = q_ref.shape[1] // (group * width)
    bias = bias_ref[...]
    for h in range(heads):
        k = kv_ref[:, h * width : (h + 1) * width]
        v = kv_ref[:, (heads + h) * width : (heads + h + 1) * width]
        for g in range(h * group, (h + 1) * group):
            cols = slice(g * width, (g + 1) * width)
            scores = lax.dot_general(
                q_ref[:, cols], k, (((1,), (1,)), ((), ())), preferred_element_type=jnp.float32
            )
            scores = scores * scale + bias
            expo = jnp.exp(scores - jnp.max(scores, axis=-1, keepdims=True))
            total = jnp.sum(expo, axis=-1, keepdims=True)
            product = jnp.dot(expo.astype(jnp.bfloat16), v, preferred_element_type=jnp.float32)
            out_ref[:, cols] = (product / total).astype(jnp.bfloat16)


def local_attention(scale, queries, piece, visible):
    return pl.pallas_call(
        functools.partial(attention_kernel, scale),
        out_shape=jax.ShapeDtypeStruct(queries.shape, jnp.bfloat16),
        in_specs=[VMEM_REF] * 3,
        out_specs=VMEM_REF,
        compiler_params=pltpu.CompilerParams(vmem_limit_bytes=40 * MIB),
    )(queries, piece, jnp.where(visible, 0.0, NEG))


def weight_chunk(w_ref, wbuf, sem, origin, slot):
    depth = wbuf.shape[2]
    rows = pl.ds(pl.multiple_of(origin * depth, depth), depth)
    return pltpu.make_async_copy(w_ref.at[:, rows, :], wbuf.at[slot], sem.at[slot])


def hidden_kernel(width, x_ref, gain_ref, gate_ref, up_ref, out_ref, buf, wg, wu, ag, au, ss, wsem_g, wsem_u, *sems):
    experts = buf.shape[1]

    def fetch(origin, slot):
        weight_chunk(gate_ref, wg, wsem_g, origin, slot).start()
        weight_chunk(up_ref, wu, wsem_u, origin, slot).start()

    def consume(step, origin, following):
        slot = step % 2
        weight_chunk(gate_ref, wg, wsem_g, origin, slot).wait()
        weight_chunk(up_ref, wu, wsem_u, origin, slot).wait()
        if following is not None:
            fetch(following, 1 - slot)
        gain = gain_ref[origin]

        def one(e, carry):
            xf = buf[origin, e].astype(jnp.float32)
            xg = (xf * gain).astype(jnp.bfloat16)
            squares = jnp.sum(xf * xf, axis=-1, keepdims=True)
            g = jnp.dot(xg, wg[slot, e], preferred_element_type=jnp.float32)
            u = jnp.dot(xg, wu[slot, e], preferred_element_type=jnp.float32)
            if step == 0:
                ss[e] = squares
                ag[e] = g
                au[e] = u
            else:
                ss[e] += squares
                ag[e] += g
                au[e] += u
            return carry

        lax.fori_loop(0, experts, one, 0)

    ring_gather(x_ref, buf, sems, consume, lambda me: fetch(me, 0))

    def finish(e, carry):
        inverse = lax.rsqrt(ss[e] / width + 1e-05)
        g = ag[e] * inverse
        u = au[e] * inverse
        out_ref[e] = (g / (1.0 + jnp.exp(-g)) * u).astype(out_ref.dtype)
        return carry

    lax.fori_loop(0, experts, finish, 0)


def ring_hidden(rows, gain, gate_proj, up_proj):
    experts, count, depth = rows.shape
    units = gate_proj.shape[2]
    return pl.pallas_call(
        functools.partial(hidden_kernel, gate_proj.shape[1]),
        out_shape=jax.ShapeDtypeStruct((experts, count, units), jnp.bfloat16),
        in_specs=[ANY_REF, VMEM_REF, ANY_REF, ANY_REF],
        out_specs=VMEM_REF,
        scratch_shapes=[
            pltpu.VMEM((RING_SIZE, experts, count, depth), jnp.bfloat16),
            pltpu.VMEM((2, experts, depth, units), jnp.bfloat16),
            pltpu.VMEM((2, experts, depth, units), jnp.bfloat16),
            pltpu.VMEM((experts, count, units), jnp.float32),
            pltpu.VMEM((experts, count, units), jnp.float32),
            pltpu.VMEM((experts, count, 1), jnp.float32),
            pltpu.SemaphoreType.DMA((2,)),
            pltpu.SemaphoreType.DMA((2,)),
        ]
        + RING_SEMS,
        compiler_params=pltpu.CompilerParams(
            collective_id=2, has_side_effects=True, vmem_limit_bytes=48 * MIB
        ),
    )(rows, gain, gate_proj, up_proj)


def down_kernel(x_ref, down_ref, out_ref, buf, wd, wsem, *sems):
    experts = buf.shape[1]

    def consume(step, origin, following):
        slot = step % 2
        weight_chunk(down_ref, wd, wsem, origin, slot).wait()
        if following is not None:
            weight_chunk(down_ref, wd, wsem, following, 1 - slot).start()

        def one(e, carry):
            y = jnp.dot(buf[origin, e], wd[slot, e], preferred_element_type=jnp.float32)
            if step == 0:
                out_ref[e] = y
            else:
                out_ref[e] += y
            return carry

        lax.fori_loop(0, experts, one, 0)

    ring_gather(
        x_ref, buf, sems, consume, lambda me: weight_chunk(down_ref, wd, wsem, me, 0).start()
    )


def ring_down(hidden, down_proj):
    experts, count, depth = hidden.shape
    features = down_proj.shape[2]
    return pl.pallas_call(
        down_kernel,
        out_shape=jax.ShapeDtypeStruct((experts, count, features), jnp.float32),
        in_specs=[ANY_REF, ANY_REF],
        out_specs=VMEM_REF,
        scratch_shapes=[
            pltpu.VMEM((RING_SIZE, experts, count, depth), jnp.bfloat16),
            pltpu.VMEM((2, experts, depth, features), jnp.bfloat16),
            pltpu.SemaphoreType.DMA((2,)),
        ]
        + RING_SEMS,
        compiler_params=pltpu.CompilerParams(
            collective_id=3, has_side_effects=True, vmem_limit_bytes=48 * MIB
        ),
    )(hidden, down_proj)


def slot_ranks(expert_ids, n_experts, n_blocks):
    seq_len = expert_ids.shape[0]
    rows_block = seq_len // n_blocks
    labels = jnp.arange(n_experts, dtype=jnp.int32)
    onehot = (expert_ids[:, :, None] == labels[None, None, :]).astype(jnp.int32)
    hits = jnp.sum(onehot, axis=1).reshape(n_blocks, rows_block, n_experts)
    before = (jnp.cumsum(hits, axis=1) - hits).reshape(seq_len, n_experts)
    return jnp.sum(onehot * before[:, None, :], axis=2)


def on_device(
    ring,
    queries,
    projected_key_value,
    doc_ids,
    residual_in,
    out_proj,
    norm_gain,
    expert_ids,
    route_weights,
    gate_proj,
    up_proj,
    down_proj,
):
    tok_count = queries.shape[0]
    head_groups = QUERY_HEADS // KEY_VALUE_HEADS
    kv_width = projected_key_value.shape[2]
    kv_local = kv_width // HEAD_WIDTH
    scale = 1.0 / math.sqrt(HEAD_WIDTH)
    heads_of_queries = queries.reshape(tok_count, kv_local, head_groups, HEAD_WIDTH)
    query_pos = lax.axis_index("ctx") * tok_count + jnp.arange(tok_count, dtype=jnp.int32)

    feat_local = norm_gain.shape[0]
    per_row = -(-feat_local // tok_count)
    gain_cols = jnp.pad(norm_gain, (0, per_row * tok_count - feat_local)).reshape(tok_count, per_row)
    side = jnp.concatenate([doc_ids.astype(jnp.bfloat16)[:, None], gain_cols], axis=1)
    side = jnp.pad(side, ((0, 0), (0, HEAD_WIDTH - 1 - per_row)))
    packed = jnp.concatenate([projected_key_value.reshape(tok_count, 2 * kv_width), side], axis=1)
    piece = gathered_rows(packed) if ring else lax.all_gather(packed, "ctx", axis=0, tiled=True)
    key_rows = piece.shape[0]
    ctx_size = key_rows // tok_count
    doc_piece = piece[:, 2 * kv_width].astype(jnp.int32)
    gain_piece = piece[:, 2 * kv_width + 1 : 2 * kv_width + 1 + per_row]
    gain_full = gain_piece.reshape(ctx_size, tok_count * per_row)[:, :feat_local].astype(jnp.float32)
    heads_of_keys = piece[:, :kv_width].reshape(key_rows, kv_local, HEAD_WIDTH)
    heads_of_values = piece[:, kv_width : 2 * kv_width].reshape(key_rows, kv_local, HEAD_WIDTH)
    key_pos = jnp.arange(key_rows, dtype=jnp.int32)
    visible = (doc_ids[:, None] == doc_piece[None, :]) & (key_pos[None, :] <= query_pos[:, None])
    if ring:
        attended = local_attention(scale, queries, piece, visible)
        partial_out = ring_project(attended, out_proj)
    else:
        scores = (
            jnp.einsum(
                "tkgd,skd->kgts", heads_of_queries, heads_of_keys, preferred_element_type=jnp.float32
            )
            * scale
        )
        scores = jnp.where(visible, scores, NEG)
        top = jnp.max(scores, axis=-1)
        expo = jnp.where(visible, jnp.exp(scores - top[..., None]), 0.0)
        total_new = jnp.sum(expo, axis=-1)
        weights = expo.astype(jnp.bfloat16)
        product = jnp.einsum(
            "kgts,skd->kgtd", weights, heads_of_values, preferred_element_type=jnp.float32
        )
        attended = (
            (product / total_new[..., None])
            .transpose(2, 0, 1, 3)
            .reshape(tok_count, -1)
            .astype(jnp.bfloat16)
        )
        partial_out = jnp.dot(
            lax.all_gather(attended, "ctx", axis=0, tiled=True),
            out_proj,
            preferred_element_type=jnp.float32,
        )

    n_blocks = lax.axis_size("exp")
    block_index = lax.axis_index("exp")
    seq_len = expert_ids.shape[0]
    rows_block = seq_len // n_blocks
    capacity = rows_block * 9 // 32
    width = n_blocks * capacity
    local_experts = gate_proj.shape[0]
    rank = slot_ranks(expert_ids, EXPERTS, n_blocks)
    position = jnp.arange(seq_len, dtype=jnp.int32)
    slot_key = expert_ids * width + (position // rows_block)[:, None] * capacity + rank
    own_rows = lax.dynamic_slice_in_dim(
        partial_out, block_index * rows_block, rows_block, 0
    ) + residual_in.astype(jnp.float32)
    with_base = lax.dynamic_update_slice_in_dim(
        partial_out, own_rows, block_index * rows_block, 0
    ).astype(jnp.bfloat16)
    slots = jnp.arange(EXPERTS * width, dtype=jnp.int32)[:, None]
    chosen = ((slots == slot_key[None, :, 0]) | (slots == slot_key[None, :, 1])).astype(jnp.bfloat16)
    shares = jnp.dot(chosen, with_base, preferred_element_type=jnp.float32)
    received = lax.all_to_all(
        shares.astype(jnp.bfloat16).reshape(EXPERTS, width, feat_local),
        "exp",
        split_axis=0,
        concat_axis=1,
        tiled=True,
    ).astype(jnp.float32)
    expert_rows = jnp.sum(
        received.reshape(local_experts, n_blocks, -1, feat_local), axis=1
    ).astype(jnp.bfloat16)

    my_slots = block_index * local_experts * width + jnp.arange(local_experts * width, dtype=jnp.int32)
    lead = my_slots[:, None] == slot_key[None, :, 0]
    second = my_slots[:, None] == slot_key[None, :, 1]
    my_weight = jnp.sum(
        jnp.where(lead, route_weights[None, :, 0], jnp.where(second, route_weights[None, :, 1], 0.0)),
        axis=1,
    ).reshape(local_experts, width)
    my_first = jnp.sum(lead.astype(jnp.float32), axis=1).reshape(local_experts, width)

    if ring:
        hidden = ring_hidden(expert_rows, gain_full[:, None, :], gate_proj, up_proj)
        expert_out = ring_down(hidden, down_proj)
    else:
        full_rows = lax.all_gather(expert_rows, "ctx", axis=2, tiled=True)
        meansq = (
            jnp.einsum("erd,erd->er", full_rows, full_rows, preferred_element_type=jnp.float32)
            / full_rows.shape[2]
        )
        inverse = lax.rsqrt(meansq + 1e-05)
        normed = (
            full_rows.astype(jnp.float32) * inverse[..., None] * gain_full.reshape(-1)
        ).astype(jnp.bfloat16)
        gate = jnp.einsum("erd,edf->erf", normed, gate_proj, preferred_element_type=jnp.float32)
        upper = jnp.einsum("erd,edf->erf", normed, up_proj, preferred_element_type=jnp.float32)
        hidden = (jax.nn.silu(gate) * upper).astype(jnp.bfloat16)
        expert_out = jnp.einsum(
            "erf,efd->erd",
            lax.all_gather(hidden, "ctx", axis=2, tiled=True),
            down_proj,
            preferred_element_type=jnp.float32,
        )
    payload = my_weight[..., None] * expert_out + my_first[..., None] * expert_rows.astype(
        jnp.float32
    )
    back = lax.all_to_all(
        payload.reshape(local_experts, n_blocks, capacity, feat_local).astype(jnp.bfloat16),
        "exp",
        split_axis=1,
        concat_axis=0,
        tiled=True,
    )
    back = back.reshape(EXPERTS * capacity, feat_local)
    block_key = lax.dynamic_slice_in_dim(
        expert_ids * capacity + rank, block_index * rows_block, rows_block, 0
    )
    labels = jnp.arange(EXPERTS * capacity, dtype=jnp.int32)[None, :]
    picker = ((labels == block_key[:, :1]) | (labels == block_key[:, 1:])).astype(jnp.bfloat16)
    mixed = jnp.dot(picker, back, preferred_element_type=jnp.float32)
    return mixed.astype(jnp.bfloat16)


def solution(mesh):
    ring = mesh.shape["ctx"] == RING_SIZE
    placed = (
        P("ctx", "exp"),
        P("ctx", None, "exp"),
        P("ctx"),
        P("exp", "ctx"),
        P("exp", "ctx"),
        P("ctx"),
        P(),
        P(),
        P("exp", None, "ctx"),
        P("exp", None, "ctx"),
        P("exp", None, "ctx"),
    )
    return jax.shard_map(
        functools.partial(on_device, ring),
        mesh=mesh,
        in_specs=placed,
        out_specs=P("exp", "ctx"),
        check_vma=False,
    )
```

```python
import functools
import math

import jax
import jax.numpy as jnp
from jax import lax
from jax.experimental import pallas as pl
from jax.experimental.pallas import tpu as pltpu
from jax.sharding import PartitionSpec as P

QUERY_HEADS = 48
KEY_VALUE_HEADS = 8
HEAD_WIDTH = 128
EXPERTS = 8
NEG = -1e30

CHIPS = 8
RING_SIZE = 2 * CHIPS
MIB = 1 << 20


def chip_of(pos):
    x = pos // 4
    z = pos * (1 - x) + (CHIPS - 1 - pos) * x
    return z * 2 + x


def ring_place():
    me = lax.axis_index("ctx")
    core = lax.rem(me, 2)
    x = lax.rem(me // 2, 2)
    z = me // 4
    return z * (1 - x) + (CHIPS - 1 - z) * x, core


def ring_gather(x_ref, buf, sems, consume=None, ahead=None):
    local_sem, send_r, recv_r, send_l, recv_l, send_s, recv_s = sems
    pos, core = ring_place()

    def at(offset, c):
        return chip_of(lax.rem(pos + offset + CHIPS, CHIPS)) * 2 + c

    me = at(0, core)
    right, left, sibling = at(1, core), at(-1, core), at(0, 1 - core)
    half = x_ref.shape[0] // 2

    own = pltpu.make_async_copy(x_ref, buf.at[me], local_sem)
    own.start()
    barrier = pltpu.get_barrier_semaphore()
    for other in (right, left, sibling):
        pl.semaphore_signal(
            barrier, inc=1, device_id={"ctx": other}, device_id_type=pl.DeviceIdType.MESH
        )
    if ahead is not None:
        ahead(me)
    pl.semaphore_wait(barrier, 3)
    own.wait()

    def copy(origin, target, send, recv, part=None):
        view = buf.at[origin]
        if part is not None:
            view = buf.at[origin, pl.ds(part * half, half)]
        return pltpu.make_async_remote_copy(
            src_ref=view,
            dst_ref=view,
            send_sem=send,
            recv_sem=recv,
            device_id={"ctx": target},
            device_id_type=pl.DeviceIdType.MESH,
        )

    def rightward(k, part, sent):
        n = 2 * (k - 1) + part
        return copy(at(1 - k if sent else -k, core), right, send_r.at[n], recv_r.at[n], part)

    def leftward(k, part, sent):
        n = 2 * (k - 1) + part
        return copy(at(k - 1 if sent else k, core), left, send_l.at[n], recv_l.at[n], part)

    def to_sibling(n, offset):
        return copy(at(offset, core), sibling, send_s.at[n], recv_s.at[n])

    def from_sibling(n, offset):
        return copy(at(offset, 1 - core), sibling, send_s.at[n], recv_s.at[n])

    order = [(0, 0), (-1, 0), (1, 0), (0, 1)]
    order += [(-2, 0), (2, 0), (-1, 1), (1, 1)]
    order += [(-3, 0), (3, 0), (-2, 1), (2, 1), (-3, 1), (3, 1), (4, 0), (4, 1)]
    number = {0: 0, -1: 1, 1: 2, -2: 3, 2: 4, -3: 5, 3: 6, 4: 7}

    def place(step):
        offset, other = order[step]
        return at(offset, 1 - core if other else core)

    def use(step):
        offset, other = order[step]
        if other:
            from_sibling(number[offset], offset).wait_recv()
        if consume is not None:
            consume(step, place(step), place(step + 1) if step + 1 < len(order) else None)

    rightward(1, 0, True).start()
    leftward(1, 1, True).start()
    rightward(1, 1, True).start()
    leftward(1, 0, True).start()
    to_sibling(0, 0).start()
    before = {1: (0,), 2: (1, 2), 3: (4, 5)}
    between = {1: (), 2: (3,), 3: (6, 7)}
    for k in (1, 2, 3):
        for step in before[k]:
            use(step)
        rightward(k, 0, False).wait_recv()
        rightward(k + 1, 0, True).start()
        leftward(k, 1, False).wait_recv()
        leftward(k + 1, 1, True).start()
        for step in between[k]:
            use(step)
        rightward(k, 1, False).wait_recv()
        if k < 3:
            rightward(k + 1, 1, True).start()
        to_sibling(number[-k], -k).start()
        leftward(k, 0, False).wait_recv()
        if k < 3:
            leftward(k + 1, 0, True).start()
        to_sibling(number[k], k).start()
    for step in (8, 9, 10, 11):
        use(step)
    rightward(4, 0, False).wait_recv()
    leftward(4, 1, False).wait_recv()
    to_sibling(7, 4).start()
    for step in (12, 13, 14, 15):
        use(step)
    for k in (1, 2, 3, 4):
        rightward(k, 0, True).wait_send()
        leftward(k, 1, True).wait_send()
        if k < 4:
            rightward(k, 1, True).wait_send()
            leftward(k, 0, True).wait_send()
    for offset, n in number.items():
        to_sibling(n, offset).wait_send()


RING_SEMS = [
    pltpu.SemaphoreType.DMA,
    pltpu.SemaphoreType.DMA((8,)),
    pltpu.SemaphoreType.DMA((8,)),
    pltpu.SemaphoreType.DMA((8,)),
    pltpu.SemaphoreType.DMA((8,)),
    pltpu.SemaphoreType.DMA((8,)),
    pltpu.SemaphoreType.DMA((8,)),
]
VMEM_REF = pl.BlockSpec(memory_space=pltpu.VMEM)
ANY_REF = pl.BlockSpec(memory_space=pl.ANY)


def gather_kernel(x_ref, out_ref, *sems):
    ring_gather(x_ref, out_ref, sems)


def gathered_rows(x):
    out = pl.pallas_call(
        gather_kernel,
        out_shape=jax.ShapeDtypeStruct((RING_SIZE,) + x.shape, x.dtype),
        in_specs=[ANY_REF],
        out_specs=VMEM_REF,
        scratch_shapes=RING_SEMS,
        compiler_params=pltpu.CompilerParams(
            collective_id=0, has_side_effects=True, vmem_limit_bytes=16 * MIB
        ),
    )(x)
    return out.reshape((RING_SIZE * x.shape[0],) + x.shape[1:])


def project_kernel(x_ref, w_ref, out_ref, buf, *sems):
    ring_gather(x_ref, buf, sems)
    shards = 4
    rows = shards * x_ref.shape[0]
    for group in range(RING_SIZE // shards):
        x = buf[pl.ds(group * shards, shards)].reshape(rows, x_ref.shape[1])
        out_ref[pl.ds(group * rows, rows), :] = jnp.dot(
            x, w_ref[...], preferred_element_type=jnp.float32
        )


def ring_project(x, weight):
    return pl.pallas_call(
        project_kernel,
        out_shape=jax.ShapeDtypeStruct((RING_SIZE * x.shape[0], weight.shape[1]), jnp.float32),
        in_specs=[ANY_REF, VMEM_REF],
        out_specs=VMEM_REF,
        scratch_shapes=[pltpu.VMEM((RING_SIZE,) + x.shape, x.dtype)] + RING_SEMS,
        compiler_params=pltpu.CompilerParams(
            collective_id=1, has_side_effects=True, vmem_limit_bytes=40 * MIB
        ),
    )(x, weight)


def attention_kernel(scale, q_ref, kv_ref, bias_ref, out_ref):
    count, width = q_ref.shape[0], HEAD_WIDTH
    group = QUERY_HEADS // KEY_VALUE_HEADS
    heads = q_ref.shape[1] // (group * width)
    bias = bias_ref[...]
    for h in range(heads):
        k = kv_ref[:, h * width : (h + 1) * width]
        v = kv_ref[:, (heads + h) * width : (heads + h + 1) * width]
        for g in range(h * group, (h + 1) * group):
            cols = slice(g * width, (g + 1) * width)
            scores = lax.dot_general(
                q_ref[:, cols], k, (((1,), (1,)), ((), ())), preferred_element_type=jnp.float32
            )
            scores = scores * scale + bias
            expo = jnp.exp(scores - jnp.max(scores, axis=-1, keepdims=True))
            total = jnp.sum(expo, axis=-1, keepdims=True)
            product = jnp.dot(expo.astype(jnp.bfloat16), v, preferred_element_type=jnp.float32)
            out_ref[:, cols] = (product / total).astype(jnp.bfloat16)


def local_attention(scale, queries, piece, visible):
    return pl.pallas_call(
        functools.partial(attention_kernel, scale),
        out_shape=jax.ShapeDtypeStruct(queries.shape, jnp.bfloat16),
        in_specs=[VMEM_REF] * 3,
        out_specs=VMEM_REF,
        compiler_params=pltpu.CompilerParams(vmem_limit_bytes=40 * MIB),
    )(queries, piece, jnp.where(visible, 0.0, NEG))


def weight_chunk(w_ref, wbuf, sem, origin, slot):
    depth = wbuf.shape[2]
    rows = pl.ds(pl.multiple_of(origin * depth, depth), depth)
    return pltpu.make_async_copy(w_ref.at[:, rows, :], wbuf.at[slot], sem.at[slot])


def hidden_kernel(width, x_ref, gain_ref, gate_ref, up_ref, out_ref, buf, wg, wu, ag, au, ss, wsem_g, wsem_u, *sems):
    experts = buf.shape[1]

    def fetch(origin, slot):
        weight_chunk(gate_ref, wg, wsem_g, origin, slot).start()
        weight_chunk(up_ref, wu, wsem_u, origin, slot).start()

    def consume(step, origin, following):
        slot = step % 2
        weight_chunk(gate_ref, wg, wsem_g, origin, slot).wait()
        weight_chunk(up_ref, wu, wsem_u, origin, slot).wait()
        if following is not None:
            fetch(following, 1 - slot)
        gain = gain_ref[origin]

        def one(e, carry):
            xf = buf[origin, e].astype(jnp.float32)
            xg = (xf * gain).astype(jnp.bfloat16)
            squares = jnp.sum(xf * xf, axis=-1, keepdims=True)
            g = jnp.dot(xg, wg[slot, e], preferred_element_type=jnp.float32)
            u = jnp.dot(xg, wu[slot, e], preferred_element_type=jnp.float32)
            if step == 0:
                ss[e] = squares
                ag[e] = g
                au[e] = u
            else:
                ss[e] += squares
                ag[e] += g
                au[e] += u
            return carry

        lax.fori_loop(0, experts, one, 0, unroll=2)

    ring_gather(x_ref, buf, sems, consume, lambda me: fetch(me, 0))

    def finish(e, carry):
        inverse = lax.rsqrt(ss[e] / width + 1e-05)
        g = ag[e] * inverse
        u = au[e] * inverse
        out_ref[e] = (g / (1.0 + jnp.exp(-g)) * u).astype(out_ref.dtype)
        return carry

    lax.fori_loop(0, experts, finish, 0)


def ring_hidden(rows, gain, gate_proj, up_proj):
    experts, count, depth = rows.shape
    units = gate_proj.shape[2]
    return pl.pallas_call(
        functools.partial(hidden_kernel, gate_proj.shape[1]),
        out_shape=jax.ShapeDtypeStruct((experts, count, units), jnp.bfloat16),
        in_specs=[ANY_REF, VMEM_REF, ANY_REF, ANY_REF],
        out_specs=VMEM_REF,
        scratch_shapes=[
            pltpu.VMEM((RING_SIZE, experts, count, depth), jnp.bfloat16),
            pltpu.VMEM((2, experts, depth, units), jnp.bfloat16),
            pltpu.VMEM((2, experts, depth, units), jnp.bfloat16),
            pltpu.VMEM((experts, count, units), jnp.float32),
            pltpu.VMEM((experts, count, units), jnp.float32),
            pltpu.VMEM((experts, count, 1), jnp.float32),
            pltpu.SemaphoreType.DMA((2,)),
            pltpu.SemaphoreType.DMA((2,)),
        ]
        + RING_SEMS,
        compiler_params=pltpu.CompilerParams(
            collective_id=2, has_side_effects=True, vmem_limit_bytes=48 * MIB
        ),
    )(rows, gain, gate_proj, up_proj)


def down_kernel(x_ref, down_ref, out_ref, buf, wd, wsem, *sems):
    experts = buf.shape[1]

    def consume(step, origin, following):
        slot = step % 2
        weight_chunk(down_ref, wd, wsem, origin, slot).wait()
        if following is not None:
            weight_chunk(down_ref, wd, wsem, following, 1 - slot).start()

        def one(e, carry):
            y = jnp.dot(buf[origin, e], wd[slot, e], preferred_element_type=jnp.float32)
            if step == 0:
                out_ref[e] = y
            else:
                out_ref[e] += y
            return carry

        lax.fori_loop(0, experts, one, 0)

    ring_gather(
        x_ref, buf, sems, consume, lambda me: weight_chunk(down_ref, wd, wsem, me, 0).start()
    )


def ring_down(hidden, down_proj):
    experts, count, depth = hidden.shape
    features = down_proj.shape[2]
    return pl.pallas_call(
        down_kernel,
        out_shape=jax.ShapeDtypeStruct((experts, count, features), jnp.float32),
        in_specs=[ANY_REF, ANY_REF],
        out_specs=VMEM_REF,
        scratch_shapes=[
            pltpu.VMEM((RING_SIZE, experts, count, depth), jnp.bfloat16),
            pltpu.VMEM((2, experts, depth, features), jnp.bfloat16),
            pltpu.SemaphoreType.DMA((2,)),
        ]
        + RING_SEMS,
        compiler_params=pltpu.CompilerParams(
            collective_id=3, has_side_effects=True, vmem_limit_bytes=48 * MIB
        ),
    )(hidden, down_proj)


def slot_ranks(expert_ids, n_experts, n_blocks):
    seq_len = expert_ids.shape[0]
    rows_block = seq_len // n_blocks
    labels = jnp.arange(n_experts, dtype=jnp.int32)
    onehot = (expert_ids[:, :, None] == labels[None, None, :]).astype(jnp.int32)
    hits = jnp.sum(onehot, axis=1).reshape(n_blocks, rows_block, n_experts)
    before = (jnp.cumsum(hits, axis=1) - hits).reshape(seq_len, n_experts)
    return jnp.sum(onehot * before[:, None, :], axis=2)


def on_device(
    ring,
    queries,
    projected_key_value,
    doc_ids,
    residual_in,
    out_proj,
    norm_gain,
    expert_ids,
    route_weights,
    gate_proj,
    up_proj,
    down_proj,
):
    tok_count = queries.shape[0]
    head_groups = QUERY_HEADS // KEY_VALUE_HEADS
    kv_width = projected_key_value.shape[2]
    kv_local = kv_width // HEAD_WIDTH
    scale = 1.0 / math.sqrt(HEAD_WIDTH)
    heads_of_queries = queries.reshape(tok_count, kv_local, head_groups, HEAD_WIDTH)
    query_pos = lax.axis_index("ctx") * tok_count + jnp.arange(tok_count, dtype=jnp.int32)

    feat_local = norm_gain.shape[0]
    per_row = -(-feat_local // tok_count)
    gain_cols = jnp.pad(norm_gain, (0, per_row * tok_count - feat_local)).reshape(tok_count, per_row)
    side = jnp.concatenate([doc_ids.astype(jnp.bfloat16)[:, None], gain_cols], axis=1)
    side = jnp.pad(side, ((0, 0), (0, HEAD_WIDTH - 1 - per_row)))
    packed = jnp.concatenate([projected_key_value.reshape(tok_count, 2 * kv_width), side], axis=1)
    piece = gathered_rows(packed) if ring else lax.all_gather(packed, "ctx", axis=0, tiled=True)
    key_rows = piece.shape[0]
    ctx_size = key_rows // tok_count
    doc_piece = piece[:, 2 * kv_width].astype(jnp.int32)
    gain_piece = piece[:, 2 * kv_width + 1 : 2 * kv_width + 1 + per_row]
    gain_full = gain_piece.reshape(ctx_size, tok_count * per_row)[:, :feat_local].astype(jnp.float32)
    heads_of_keys = piece[:, :kv_width].reshape(key_rows, kv_local, HEAD_WIDTH)
    heads_of_values = piece[:, kv_width : 2 * kv_width].reshape(key_rows, kv_local, HEAD_WIDTH)
    key_pos = jnp.arange(key_rows, dtype=jnp.int32)
    visible = (doc_ids[:, None] == doc_piece[None, :]) & (key_pos[None, :] <= query_pos[:, None])
    if ring:
        attended = local_attention(scale, queries, piece, visible)
        partial_out = ring_project(attended, out_proj)
    else:
        scores = (
            jnp.einsum(
                "tkgd,skd->kgts", heads_of_queries, heads_of_keys, preferred_element_type=jnp.float32
            )
            * scale
        )
        scores = jnp.where(visible, scores, NEG)
        top = jnp.max(scores, axis=-1)
        expo = jnp.where(visible, jnp.exp(scores - top[..., None]), 0.0)
        total_new = jnp.sum(expo, axis=-1)
        weights = expo.astype(jnp.bfloat16)
        product = jnp.einsum(
            "kgts,skd->kgtd", weights, heads_of_values, preferred_element_type=jnp.float32
        )
        attended = (
            (product / total_new[..., None])
            .transpose(2, 0, 1, 3)
            .reshape(tok_count, -1)
            .astype(jnp.bfloat16)
        )
        partial_out = jnp.dot(
            lax.all_gather(attended, "ctx", axis=0, tiled=True),
            out_proj,
            preferred_element_type=jnp.float32,
        )

    n_blocks = lax.axis_size("exp")
    block_index = lax.axis_index("exp")
    seq_len = expert_ids.shape[0]
    rows_block = seq_len // n_blocks
    capacity = rows_block * 9 // 32
    width = n_blocks * capacity
    local_experts = gate_proj.shape[0]
    rank = slot_ranks(expert_ids, EXPERTS, n_blocks)
    position = jnp.arange(seq_len, dtype=jnp.int32)
    slot_key = expert_ids * width + (position // rows_block)[:, None] * capacity + rank
    own_rows = lax.dynamic_slice_in_dim(
        partial_out, block_index * rows_block, rows_block, 0
    ) + residual_in.astype(jnp.float32)
    with_base = lax.dynamic_update_slice_in_dim(
        partial_out, own_rows, block_index * rows_block, 0
    ).astype(jnp.bfloat16)
    slots = jnp.arange(EXPERTS * width, dtype=jnp.int32)[:, None]
    chosen = ((slots == slot_key[None, :, 0]) | (slots == slot_key[None, :, 1])).astype(jnp.bfloat16)
    shares = jnp.dot(chosen, with_base, preferred_element_type=jnp.float32)
    received = lax.all_to_all(
        shares.astype(jnp.bfloat16).reshape(EXPERTS, width, feat_local),
        "exp",
        split_axis=0,
        concat_axis=1,
        tiled=True,
    ).astype(jnp.float32)
    expert_rows = jnp.sum(
        received.reshape(local_experts, n_blocks, -1, feat_local), axis=1
    ).astype(jnp.bfloat16)

    my_slots = block_index * local_experts * width + jnp.arange(local_experts * width, dtype=jnp.int32)
    lead = my_slots[:, None] == slot_key[None, :, 0]
    second = my_slots[:, None] == slot_key[None, :, 1]
    my_weight = jnp.sum(
        jnp.where(lead, route_weights[None, :, 0], jnp.where(second, route_weights[None, :, 1], 0.0)),
        axis=1,
    ).reshape(local_experts, width)
    my_first = jnp.sum(lead.astype(jnp.float32), axis=1).reshape(local_experts, width)

    if ring:
        hidden = ring_hidden(expert_rows, gain_full[:, None, :], gate_proj, up_proj)
        expert_out = ring_down(hidden, down_proj)
    else:
        full_rows = lax.all_gather(expert_rows, "ctx", axis=2, tiled=True)
        meansq = (
            jnp.einsum("erd,erd->er", full_rows, full_rows, preferred_element_type=jnp.float32)
            / full_rows.shape[2]
        )
        inverse = lax.rsqrt(meansq + 1e-05)
        normed = (
            full_rows.astype(jnp.float32) * inverse[..., None] * gain_full.reshape(-1)
        ).astype(jnp.bfloat16)
        gate = jnp.einsum("erd,edf->erf", normed, gate_proj, preferred_element_type=jnp.float32)
        upper = jnp.einsum("erd,edf->erf", normed, up_proj, preferred_element_type=jnp.float32)
        hidden = (jax.nn.silu(gate) * upper).astype(jnp.bfloat16)
        expert_out = jnp.einsum(
            "erf,efd->erd",
            lax.all_gather(hidden, "ctx", axis=2, tiled=True),
            down_proj,
            preferred_element_type=jnp.float32,
        )
    payload = my_weight[..., None] * expert_out + my_first[..., None] * expert_rows.astype(
        jnp.float32
    )
    back = lax.all_to_all(
        payload.reshape(local_experts, n_blocks, capacity, feat_local).astype(jnp.bfloat16),
        "exp",
        split_axis=1,
        concat_axis=0,
        tiled=True,
    )
    back = back.reshape(EXPERTS * capacity, feat_local)
    block_key = lax.dynamic_slice_in_dim(
        expert_ids * capacity + rank, block_index * rows_block, rows_block, 0
    )
    labels = jnp.arange(EXPERTS * capacity, dtype=jnp.int32)[None, :]
    picker = ((labels == block_key[:, :1]) | (labels == block_key[:, 1:])).astype(jnp.bfloat16)
    mixed = jnp.dot(picker, back, preferred_element_type=jnp.float32)
    return mixed.astype(jnp.bfloat16)


def solution(mesh):
    ring = mesh.shape["ctx"] == RING_SIZE
    placed = (
        P("ctx", "exp"),
        P("ctx", None, "exp"),
        P("ctx"),
        P("exp", "ctx"),
        P("exp", "ctx"),
        P("ctx"),
        P(),
        P(),
        P("exp", None, "ctx"),
        P("exp", None, "ctx"),
        P("exp", None, "ctx"),
    )
    return jax.shard_map(
        functools.partial(on_device, ring),
        mesh=mesh,
        in_specs=placed,
        out_specs=P("exp", "ctx"),
        check_vma=False,
    )
```
